512 devices in a mesh: view: 32 (over z, x_lo), slab: 16 (over x_hi, y, core).
Axes of the slice: x: 4 (x_hi: 2, x_lo: 2; x = x_hi * 2 + x_lo), y: 4, z: 16, core: 2. Of those that a mesh axis runs over, the one named last changes fastest.
Arguments:
- projections: bfloat16 [256, 64, 736], P('view', 'slab'), may hold values from -24 to 24
- conj_index: int32 [256], P('view'), may hold values from 0 to 7
- conj_weight: float32 [256, 736], P('view'), may hold values from 0.1 to 0.9
- row_index: int32 [256, 16, 256], P('view', None, 'slab'), may hold values from 0 to 7
- col_index: int32 [256, 16384], P('view'), may hold values from 0 to 734
- col_frac: int32 [256, 16384], P('view'), may hold values from 0 to 255
Outputs:
- image: float32 [256, 16384], P('slab', 'view')
The draws below stay inside these ranges and needn't reach their ends.
All inputs are finite; a program needn't handle non-finite values.
Results may differ from the reference program's by a relative error of at most 0.0051.
Values may be sent and summed in bfloat16 or wider, within the bound.
A program may use at most 64 MiB of HBM per device.

```python
import math
import jax
import jax.numpy as jnp
from jax import lax

DC = 736
DR = 64
RIM = 2
V_DEV = 8
Z_DEV = 16
IMG_ROWS = 16
IMG_COLS = 1024
VIEWS = 256
ZS = 256
R_DEV = 4
PIX = 16384
N_VIEW = 32


def with_ends(result, stream_key, low, high):
    longest = result.shape.index(max(result.shape))
    spots = []
    for shift in (0, 1):
        where = [jax.random.randint(jax.random.fold_in(stream_key, axis), (), 0, length) for axis, length in enumerate(result.shape)]
        where[longest] = (where[longest] + shift) % result.shape[longest]
        spots.append(tuple(where))
    return result.at[spots[0]].set(low).at[spots[1]].set(high)


def steps_of(key, dims, shards, least, largest):
    gain, own = 1.0, jax.random.fold_in(key, 6)
    for dim, parts in shards:
        draws = jnp.exp(jax.random.uniform(jax.random.fold_in(own, dim), (parts,), jnp.float32, least / len(shards), largest / len(shards)))
        gain = gain * jnp.repeat(draws, dims[dim] // parts).reshape([-1 if axis == dim else 1 for axis in range(len(dims))])
    return gain


def bell_draw(stream_key, shape, scale, limit, cuts=(), held_as=jnp.bfloat16):
    entries = jax.random.normal(stream_key, shape, jnp.float32) * scale
    if len(cuts) > 0:
        entries = steps_of(stream_key, shape, cuts, -0.22, 0.18) * entries
    return jnp.clip(entries, min=-limit, max=limit).astype(held_as)


def setup_inputs(seed: int = 0) -> dict:
    splits = jax.random.split(jax.random.key(seed), 7)
    projections = bell_draw(splits[0], (VIEWS, DR, DC), 4.0, 24.0, ((0, 32), (1, 16)))
    conj_index = with_ends(jax.random.randint(splits[1], (VIEWS,), 0, V_DEV), jax.random.fold_in(splits[1], 1), 0, V_DEV - 1).astype(jnp.int32)
    conj_weight = jnp.clip(0.1 + 0.79999997 * jax.random.uniform(splits[2], (VIEWS, DC), jnp.float32) ** steps_of(splits[2], (VIEWS, DC), ((0, 32),), -0.2, 0.2), 0.1, 0.9)
    row_index = with_ends(jax.random.randint(splits[3], (VIEWS, IMG_ROWS, ZS), 0, R_DEV + 2 * RIM), jax.random.fold_in(splits[3], 1), 0, (R_DEV + 2 * RIM) - 1).astype(jnp.int32)
    col_index = with_ends(jax.random.randint(splits[4], (VIEWS, PIX), 0, DC - 1), jax.random.fold_in(splits[4], 1), 0, (DC - 1) - 1).astype(jnp.int32)
    col_frac = with_ends(jax.random.randint(splits[5], (VIEWS, PIX), 0, 256), jax.random.fold_in(splits[5], 1), 0, 255).astype(jnp.int32)
    return dict(projections=projections, conj_index=conj_index, conj_weight=conj_weight, row_index=row_index, col_index=col_index, col_frac=col_frac)


def ramp_matrix(width):
    place = jnp.arange(width, dtype=jnp.int32)
    offset = place[None, :] - place[:, None]
    square = (offset * offset).astype(jnp.float32)
    odd_term = -1.0 / (math.pi * math.pi * jnp.maximum(square, 1.0))
    values = jnp.where(offset == 0, 0.25, jnp.where(offset % 2 != 0, odd_term, 0.0))
    return values.astype(jnp.bfloat16)

def reference(projections, conj_index, conj_weight, row_index, col_index, col_frac):
    owner = jnp.arange(VIEWS, dtype=jnp.int32) // V_DEV
    partner = (owner + N_VIEW // 2) % N_VIEW * V_DEV + conj_index
    mirror = projections[partner][:, :, ::-1].astype(jnp.float32)
    weight = conj_weight[:, None, :]
    blended = ((1.0 - weight) * projections.astype(jnp.float32) + weight * mirror).astype(jnp.bfloat16)
    ramp = ramp_matrix(DC)
    filtered = jnp.einsum('vrc,cd->vrd', blended.astype(jnp.float32), ramp.astype(jnp.float32)).astype(jnp.bfloat16)
    padded = jnp.pad(filtered, ((0, 0), (RIM, RIM), (0, 0)))
    zslab = jnp.arange(ZS, dtype=jnp.int32) // Z_DEV

    def add_view(total, view_no):
        plane = padded[view_no].astype(jnp.float32)
        rows = zslab[:, None] * R_DEV + jnp.transpose(row_index[view_no])
        picked = plane[rows]
        columns = col_index[view_no].reshape(IMG_ROWS, IMG_COLS)
        fraction = col_frac[view_no].reshape(IMG_ROWS, IMG_COLS).astype(jnp.float32) / 256.0
        left_index = jnp.broadcast_to(columns[None], (ZS, IMG_ROWS, IMG_COLS))
        left = jnp.take_along_axis(picked, left_index, axis=2)
        right = jnp.take_along_axis(picked, left_index + 1, axis=2)
        value = left * (1.0 - fraction[None]) + right * fraction[None]
        return (total + value.reshape(ZS, PIX), None)
    start = jnp.zeros((ZS, PIX), jnp.float32)
    total, unused = lax.scan(add_view, start, jnp.arange(VIEWS, dtype=jnp.int32))
    return total * (1.0 / math.sqrt(VIEWS))
```

```python
import math

import jax
import jax.numpy as jnp
from jax import lax
from jax.experimental import pallas as pl
from jax.experimental.pallas import tpu as pltpu
from jax.sharding import PartitionSpec as P

MESH = pl.DeviceIdType.MESH
BF16 = jnp.bfloat16
F32 = jnp.float32

V = 8
R = 4
W = 736
NZ = 16
TILE = 1024
HALF = TILE // 2
STEP = 6
PARTS = STEP + 1
LANES = 128
LAG = 4


def iota(shape, dim):
    return lax.broadcasted_iota(jnp.int32, shape, dim)


def hat(distance):
    return jnp.maximum(1.0 - jnp.abs(distance), 0.0)


def kernel(
    conj_ref,
    proj_hbm,
    weight_hbm,
    rows_hbm,
    col_hbm,
    frac_hbm,
    out_ref,
    proj,
    weight,
    rowidx,
    col,
    frac,
    stage,
    mine,
    theirs,
    mirrored,
    mirror_weight,
    ramp,
    band,
    lhs,
    coarse,
    fine,
    pick,
    planes,
    part,
    own,
    x_out,
    x_in,
    z_out,
    z_in,
    load_sem,
    pair_sem,
    halo_send,
    halo_recv,
    x_send,
    x_recv,
    z_send,
    z_recv,
):
    view, slab = lax.axis_index("view"), lax.axis_index("slab")
    z, x_lo = view // 2, lax.rem(view, 2)
    last = lax.axis_size("slab") - 1

    def at(zz, xx):
        return (zz * 2 + xx, slab)

    def z_peer(distance):
        return lax.rem(z + distance, NZ)

    loads = [
        pltpu.make_async_copy(src, dst, load_sem.at[i])
        for i, (src, dst) in enumerate(
            ((proj_hbm, proj), (weight_hbm, weight), (rows_hbm, rowidx), (col_hbm, col), (frac_hbm, frac))
        )
    ]
    for load in loads:
        load.start()

    barrier = pltpu.get_barrier_semaphore()

    def greet(d, carry):
        pl.semaphore_signal(barrier, inc=1, device_id=at(z_peer(d), x_lo), device_id_type=MESH)
        return carry

    lax.fori_loop(1, NZ, greet, 0)
    pl.semaphore_signal(barrier, inc=1, device_id=at(z, 1 - x_lo), device_id_type=MESH)

    @pl.when(slab > 0)
    def _():
        pl.semaphore_signal(barrier, inc=1, device_id=(view, slab - 1), device_id_type=MESH)

    @pl.when(slab < last)
    def _():
        pl.semaphore_signal(barrier, inc=1, device_id=(view, slab + 1), device_id_type=MESH)

    loads[0].wait()
    for v in range(V):
        rows = proj[v].astype(F32)
        for r in range(R):
            stage[r * V + v : r * V + v + 1, :] = rows[r : r + 1]
    mine[...] = stage[...].astype(BF16)

    loads[3].wait()
    loads[4].wait()

    def prepare(tile, carry):
        off = pl.multiple_of(tile * TILE, TILE)
        k = col[:, pl.ds(off, TILE)].astype(F32)
        a = jnp.floor((k + 0.5) * (1.0 / STEP))
        place = k - a * STEP + frac[:, pl.ds(off, TILE)].astype(F32) * (1.0 / 256.0)
        for b in range(PARTS):
            fine[b, :, pl.ds(off, TILE)] = hat(place - b)
        lanes = iota((LANES, TILE), 0).astype(F32).astype(BF16)
        for v in range(V):
            coarse[v, :, pl.ds(off, TILE)] = hat(lanes - a[v : v + 1, :].astype(BF16)).astype(BF16)
        return carry

    lax.fori_loop(0, NZ // 2, prepare, 0)

    pl.semaphore_wait(
        barrier, NZ + (slab > 0).astype(jnp.int32) + (slab < last).astype(jnp.int32)
    )
    pair = pltpu.make_async_remote_copy(
        src_ref=mine,
        dst_ref=theirs,
        send_sem=pair_sem.at[0],
        recv_sem=pair_sem.at[1],
        device_id=at(z_peer(NZ // 2), x_lo),
        device_id_type=MESH,
    )
    pair.start()

    lax.fori_loop(NZ // 2, NZ, prepare, 0)

    for b in range(PARTS):
        column = STEP * iota((W, LANES), 1) + b
        offset = column + iota((W, LANES), 0) - (W - 1)
        square = (offset * offset).astype(F32)
        odd = -1.0 / (math.pi * math.pi * jnp.maximum(square, 1.0))
        value = jnp.where(offset == 0, 0.25, jnp.where((offset & 1) == 1, odd, 0.0))
        ramp[:, b * LANES : (b + 1) * LANES] = jnp.where(column < W, value, 0.0).astype(BF16)

    flip = jnp.where(iota((W, W), 0) + iota((W, W), 1) == W - 1, 1.0, 0.0).astype(BF16)
    mirrored[...] = jnp.dot(mine[...], flip, preferred_element_type=F32)
    loads[1].wait()
    whole = weight[...]
    high = whole.astype(BF16).astype(F32)
    middle = (whole - high).astype(BF16).astype(F32)
    low = (whole - high - middle).astype(BF16).astype(F32)
    split = jnp.concatenate([high, middle, low], axis=0).astype(BF16)
    flipped = jnp.dot(split, flip, preferred_element_type=F32)
    mirror_weight[...] = flipped[0:V] + flipped[V : 2 * V] + flipped[2 * V : 3 * V]

    loads[2].wait()
    for t in range(NZ):
        blocks = []
        for v in range(V):
            wanted = jnp.broadcast_to(rowidx[v, t : t + 1, :], (2 * R, NZ))
            blocks.append(jnp.where(wanted == iota((2 * R, NZ), 0), 1.0, 0.0))
        pick[t] = jnp.concatenate(blocks, axis=0).T.astype(BF16)

    row, other = iota((V * R, V * R), 0), iota((V * R, V * R), 1)
    conj = jnp.zeros((V * R, V * R), jnp.int32)
    for v in range(V):
        conj = jnp.where((row & (V - 1)) == v, conj_ref[v], conj)
    same_row = (row >> 3) == (other >> 3)
    select = jnp.where(jnp.logical_and(same_row, (other & (V - 1)) == conj), 1.0, 0.0).astype(BF16)
    share = jnp.concatenate([mirror_weight[...]] * R, axis=0)
    kept = (1.0 - share) * mirrored[...]
    pair.wait_recv()
    chosen = jnp.dot(select, theirs[...], preferred_element_type=F32)
    blended = (kept + share * chosen).astype(BF16)
    band[2 * V : (2 + R) * V, :] = jnp.dot(blended, ramp[...], preferred_element_type=F32).astype(BF16)

    halo = 2 * V
    down = pltpu.make_async_remote_copy(
        src_ref=band.at[pl.ds(halo, halo)],
        dst_ref=band.at[pl.ds(halo + R * V, halo)],
        send_sem=halo_send.at[0],
        recv_sem=halo_recv.at[0],
        device_id=(view, jnp.maximum(slab - 1, 0)),
        device_id_type=MESH,
    )
    up = pltpu.make_async_remote_copy(
        src_ref=band.at[pl.ds(2 * halo, halo)],
        dst_ref=band.at[pl.ds(0, halo)],
        send_sem=halo_send.at[1],
        recv_sem=halo_recv.at[1],
        device_id=(view, jnp.minimum(slab + 1, last)),
        device_id_type=MESH,
    )

    @pl.when(slab > 0)
    def _():
        down.start()

    @pl.when(slab < last)
    def _():
        up.start()

    @pl.when(slab == 0)
    def _():
        band[0:halo, :] = jnp.zeros((halo, PARTS * LANES), BF16)

    @pl.when(slab == last)
    def _():
        band[halo + R * V :, :] = jnp.zeros((halo, PARTS * LANES), BF16)

    @pl.when(slab < last)
    def _():
        down.wait_recv()

    @pl.when(slab > 0)
    def _():
        up.wait_recv()

    count = 2 * R * V
    to, source = iota((count, count), 0), iota((count, count), 1)
    order = jnp.where(source == (to & 7) * V + (to >> 3), 1.0, 0.0).astype(BF16)
    by_view = jnp.dot(order, band[...], preferred_element_type=F32)
    for v in range(V):
        lhs[v] = jnp.concatenate(
            [by_view[v * 2 * R : (v + 1) * 2 * R, b * LANES : (b + 1) * LANES] for b in range(PARTS)],
            axis=0,
        ).astype(BF16)

    def tile_of(n):
        return lax.rem(z + NZ // 2 + (1 - 2 * lax.rem(n, 2)) * ((n + 1) // 2), NZ)

    def x_copy(tile):
        return pltpu.make_async_remote_copy(
            src_ref=x_out.at[tile],
            dst_ref=x_in.at[tile],
            send_sem=x_send.at[tile],
            recv_sem=x_recv.at[tile],
            device_id=at(z, 1 - x_lo),
            device_id_type=MESH,
        )

    def z_copy(tile, slot):
        return pltpu.make_async_remote_copy(
            src_ref=z_out.at[tile],
            dst_ref=z_in.at[slot],
            send_sem=z_send.at[tile],
            recv_sem=z_recv.at[slot],
            device_id=at(tile, x_lo),
            device_id_type=MESH,
        )

    def compute(n):
        tile = tile_of(n)
        off = pl.multiple_of(tile * TILE, TILE)
        for v in range(V):
            columns = jnp.dot(lhs[v], coarse[v, :, pl.ds(off, TILE)], preferred_element_type=F32)
            total = None
            for b in range(PARTS):
                weights = jnp.broadcast_to(fine[b, v : v + 1, pl.ds(off, TILE)], (2 * R, TILE))
                term = columns[b * 2 * R : (b + 1) * 2 * R] * weights
                total = term if total is None else total + term
            planes[v * 2 * R : (v + 1) * 2 * R, :] = total
        part[...] = jnp.dot(pick[tile], planes[...].astype(BF16), preferred_element_type=F32)
        theirs_at = pl.multiple_of((1 - x_lo) * HALF, HALF)
        x_out[tile] = part[:, pl.ds(theirs_at, HALF)].astype(BF16)
        x_copy(tile).start()
        own[tile] = part[:, pl.ds(pl.multiple_of(x_lo * HALF, HALF), HALF)]

    def pass_on(n):
        tile = tile_of(n)
        x_copy(tile).wait_recv()
        z_out[tile] = (own[tile] + x_in[tile].astype(F32)).astype(BF16)
        z_copy(tile, z).start()

    def first(n, carry):
        compute(n)
        return carry

    def middle_steps(n, carry):
        compute(n)
        pass_on(n - LAG)
        return carry

    def tail(n, carry):
        pass_on(n)
        return carry

    lax.fori_loop(0, LAG, first, 0)
    lax.fori_loop(LAG, NZ, middle_steps, 0)
    lax.fori_loop(NZ - LAG, NZ - 1, tail, 0)
    x_copy(z).wait_recv()
    part[:, 0:HALF] = own[z] + x_in[z].astype(F32)

    def gather(d, carry):
        peer = z_peer(d)
        z_copy(peer, peer).wait_recv()
        part[:, 0:HALF] += z_in[peer].astype(F32)
        return carry

    lax.fori_loop(1, NZ, gather, 0)
    out_ref[...] = part[:, 0:HALF] * (1.0 / math.sqrt(V * lax.axis_size("view")))

    pair.wait_send()

    @pl.when(slab > 0)
    def _():
        down.wait_send()

    @pl.when(slab < last)
    def _():
        up.wait_send()

    def sent(d, carry):
        peer = z_peer(d)
        x_copy(peer).wait_send()
        z_copy(peer, z).wait_send()
        return carry

    lax.fori_loop(1, NZ, sent, 0)
    x_copy(z).wait_send()


def on_device(projections, conj_index, conj_weight, row_index, col_index, col_frac):
    pix = NZ * TILE
    anywhere = pl.BlockSpec(memory_space=pl.ANY)
    dma = pltpu.SemaphoreType.DMA
    return pl.pallas_call(
        kernel,
        out_shape=jax.ShapeDtypeStruct((NZ, HALF), F32),
        in_specs=[pl.BlockSpec(memory_space=pltpu.SMEM)] + [anywhere] * 5,
        out_specs=pl.BlockSpec(memory_space=pltpu.VMEM),
        scratch_shapes=[
            pltpu.VMEM((V, R, W), BF16),
            pltpu.VMEM((V, W), F32),
            pltpu.VMEM((V, NZ, NZ), jnp.int32),
            pltpu.VMEM((V, pix), jnp.int32),
            pltpu.VMEM((V, pix), jnp.int32),
            pltpu.VMEM((V * R, W), F32),
            pltpu.VMEM((V * R, W), BF16),
            pltpu.VMEM((V * R, W), BF16),
            pltpu.VMEM((V * R, W), F32),
            pltpu.VMEM((V, W), F32),
            pltpu.VMEM((W, PARTS * LANES), BF16),
            pltpu.VMEM((2 * R * V, PARTS * LANES), BF16),
            pltpu.VMEM((V, PARTS * 2 * R, LANES), BF16),
            pltpu.VMEM((V, LANES, pix), BF16),
            pltpu.VMEM((PARTS, V, pix), F32),
            pltpu.VMEM((NZ, NZ, 2 * R * V), BF16),
            pltpu.VMEM((2 * R * V, TILE), F32),
            pltpu.VMEM((NZ, TILE), F32),
            pltpu.VMEM((NZ, NZ, HALF), F32),
            pltpu.VMEM((NZ, NZ, HALF), BF16),
            pltpu.VMEM((NZ, NZ, HALF), BF16),
            pltpu.VMEM((NZ, NZ, HALF), BF16),
            pltpu.VMEM((NZ, NZ, HALF), BF16),
            dma((5,)),
            dma((2,)),
            dma((2,)),
            dma((2,)),
            dma((NZ,)),
            dma((NZ,)),
            dma((NZ,)),
            dma((NZ,)),
        ],
        compiler_params=pltpu.CompilerParams(
            collective_id=0, has_side_effects=True, vmem_limit_bytes=56 * 2**20
        ),
        name="backproject",
    )(conj_index, projections, conj_weight, row_index, col_index, col_frac)


def solution(mesh):
    return jax.shard_map(
        on_device,
        mesh=mesh,
        in_specs=(
            P("view", "slab", None),
            P("view"),
            P("view", None),
            P("view", None, "slab"),
            P("view", None),
            P("view", None),
        ),
        out_specs=P("slab", "view"),
        check_vma=False,
    )
```

```python
import math

import jax
import jax.numpy as jnp
from jax import lax
from jax.experimental import pallas as pl
from jax.experimental.pallas import tpu as pltpu
from jax.sharding import PartitionSpec as P

MESH = pl.DeviceIdType.MESH
BF16 = jnp.bfloat16
F32 = jnp.float32

V = 8
R = 4
W = 736
NZ = 16
TILE = 1024
HALF = TILE // 2
STEP = 6
PARTS = STEP + 1
LANES = 128
REACH = 4
FAR = NZ // 2 - 1


def iota(shape, dim):
    return lax.broadcasted_iota(jnp.int32, shape, dim)


def hat(distance):
    return jnp.maximum(1.0 - jnp.abs(distance), 0.0)


def kernel(
    conj_hbm,
    proj_hbm,
    weight_hbm,
    rows_hbm,
    col_hbm,
    frac_hbm,
    out_ref,
    conj_ref,
    proj,
    weight,
    rowidx,
    col,
    frac,
    stage,
    mine,
    theirs,
    kept,
    mirror_weight,
    ramp,
    edge,
    edge_in,
    band,
    lhs,
    coarse,
    fine,
    pick,
    planes,
    part,
    own,
    block,
    x_in,
    relay_in,
    z_in,
    load_sem,
    pair_sem,
    halo_send,
    halo_recv,
    block_send,
    x_recv,
    relay_recv,
    z_recv,
):
    view, slab = lax.axis_index("view"), lax.axis_index("slab")
    z, x_lo = view // 2, lax.rem(view, 2)
    last = lax.axis_size("slab") - 1

    def at(zz, xx):
        return (zz * 2 + xx, slab)

    def z_peer(distance):
        return lax.rem(z + distance, NZ)

    barrier = pltpu.get_barrier_semaphore()

    def greet(*device):
        pl.semaphore_signal(barrier, inc=1, device_id=device, device_id_type=MESH)

    def greet_z(d, carry):
        for x in range(2):
            greet(*at(z_peer(d), x))
            greet(*at(z_peer(NZ - d), x))
        return carry

    partner = at(z_peer(NZ // 2), x_lo)
    greet(*partner)
    lax.fori_loop(1, REACH + 1, greet_z, 0)
    greet(*at(z, 1 - x_lo))

    @pl.when(slab > 0)
    def _():
        greet(view, slab - 1)

    @pl.when(slab < last)
    def _():
        greet(view, slab + 1)

    loads = [
        pltpu.make_async_copy(src, dst, load_sem.at[i])
        for i, (src, dst) in enumerate(
            (
                (proj_hbm, proj),
                (weight_hbm, weight),
                (rows_hbm, rowidx),
                (col_hbm, col),
                (frac_hbm, frac),
                (conj_hbm, conj_ref),
            )
        )
    ]
    for load in loads:
        load.start()

    loads[0].wait()
    for v in range(V):
        rows = proj[v].astype(F32)
        for r in range(R):
            stage[r * V + v : r * V + v + 1, :] = rows[r : r + 1]
    mine[...] = stage[...].astype(BF16)

    loads[3].wait()
    loads[4].wait()

    def prepare(tile, carry):
        off = pl.multiple_of(tile * TILE, TILE)
        k = col[:, pl.ds(off, TILE)].astype(F32)
        a = jnp.floor((k + 0.5) * (1.0 / STEP))
        place = k - a * STEP + frac[:, pl.ds(off, TILE)].astype(F32) * (1.0 / 256.0)
        for b in range(PARTS):
            fine[b, :, pl.ds(off, TILE)] = hat(place - b)
        lanes = iota((LANES, TILE), 0).astype(F32).astype(BF16)
        for v in range(V):
            coarse[v, :, pl.ds(off, TILE)] = hat(lanes - a[v : v + 1, :].astype(BF16)).astype(BF16)
        return carry

    early = jnp.where(z < 8, 12, jnp.where(z < 12, 2, 7))
    lax.fori_loop(0, early, prepare, 0)

    below, above = (slab > 0).astype(jnp.int32), (slab < last).astype(jnp.int32)
    pl.semaphore_wait(barrier, 4 * REACH + 2 + below + above)
    pair = pltpu.make_async_remote_copy(
        src_ref=mine,
        dst_ref=theirs,
        send_sem=pair_sem.at[0],
        recv_sem=pair_sem.at[1],
        device_id=partner,
        device_id_type=MESH,
    )
    pair.start()
    lax.fori_loop(early, NZ, prepare, 0)

    for b in range(PARTS):
        column = STEP * iota((W, LANES), 1) + b
        offset = column + iota((W, LANES), 0) - (W - 1)
        square = (offset * offset).astype(F32)
        odd = -1.0 / (math.pi * math.pi * jnp.maximum(square, 1.0))
        value = jnp.where(offset == 0, 0.25, jnp.where((offset & 1) == 1, odd, 0.0))
        ramp[:, b * LANES : (b + 1) * LANES] = jnp.where(column < W, value, 0.0).astype(BF16)

    flip = jnp.where(iota((W, W), 0) + iota((W, W), 1) == W - 1, 1.0, 0.0).astype(BF16)
    loads[1].wait()
    whole = weight[...]
    high = whole.astype(BF16).astype(F32)
    middle = (whole - high).astype(BF16).astype(F32)
    low = (whole - high - middle).astype(BF16).astype(F32)
    split = jnp.concatenate([high, middle, low], axis=0).astype(BF16)
    flipped = jnp.dot(split, flip, preferred_element_type=F32)
    mirror_weight[...] = flipped[0:V] + flipped[V : 2 * V] + flipped[2 * V : 3 * V]
    share = jnp.concatenate([mirror_weight[...]] * R, axis=0)

    kept[...] = (1.0 - share) * jnp.dot(mine[...], flip, preferred_element_type=F32)

    loads[2].wait()
    for t in range(NZ):
        blocks = []
        for v in range(V):
            wanted = jnp.broadcast_to(rowidx[v, t : t + 1, :], (2 * R, NZ))
            blocks.append(jnp.where(wanted == iota((2 * R, NZ), 0), 1.0, 0.0))
        pick[t] = jnp.concatenate(blocks, axis=0).T.astype(BF16)

    row, other = iota((V * R, V * R), 0), iota((V * R, V * R), 1)
    conj = jnp.zeros((V * R, V * R), jnp.int32)
    loads[5].wait()
    for v in range(V):
        conj = jnp.where((row & (V - 1)) == v, conj_ref[v], conj)
    same_row = (row >> 3) == (other >> 3)
    select = jnp.where(jnp.logical_and(same_row, (other & (V - 1)) == conj), 1.0, 0.0).astype(BF16)
    pair.wait_recv()
    chosen = jnp.dot(select, theirs[...], preferred_element_type=F32)
    blended = (kept[...] + share * chosen).astype(BF16)
    edge[...] = jnp.dot(blended, ramp[...], preferred_element_type=F32).astype(BF16)

    half = R * V // 2
    first_rows, last_rows = pl.ds(0, half), pl.ds(half, half)

    def halo_copy(i, src, dst, to):
        return pltpu.make_async_remote_copy(
            src_ref=edge.at[src],
            dst_ref=edge_in.at[dst],
            send_sem=halo_send.at[i],
            recv_sem=halo_recv.at[i],
            device_id=(view, to),
            device_id_type=MESH,
        )

    down = halo_copy(0, first_rows, last_rows, jnp.maximum(slab - 1, 0))
    up = halo_copy(1, last_rows, first_rows, jnp.minimum(slab + 1, last))

    @pl.when(slab > 0)
    def _():
        down.start()

    @pl.when(slab < last)
    def _():
        up.start()

    @pl.when(slab == 0)
    def _():
        edge_in[first_rows, :] = jnp.zeros((half, PARTS * LANES), BF16)

    @pl.when(slab == last)
    def _():
        edge_in[last_rows, :] = jnp.zeros((half, PARTS * LANES), BF16)

    inner = edge[...].astype(F32)
    for b in range(PARTS):
        band[b, half : half + R * V, :] = inner[:, b * LANES : (b + 1) * LANES]

    @pl.when(slab < last)
    def _():
        down.wait_recv()

    @pl.when(slab > 0)
    def _():
        up.wait_recv()

    outer = edge_in[...].astype(F32)
    for b in range(PARTS):
        band[b, 0:half, :] = outer[0:half, b * LANES : (b + 1) * LANES]
        band[b, half + R * V :, :] = outer[half:, b * LANES : (b + 1) * LANES]

    for v in range(V):
        lhs[v] = jnp.concatenate(
            [band[b, pl.ds(v, 2 * R, stride=V), :] for b in range(PARTS)], axis=0
        ).astype(BF16)

    def way(n):
        return 1 - 2 * lax.rem(n, 2)

    def distance(n):
        return NZ // 2 - (n + 1) // 2

    def tile_of(n):
        return lax.rem(z + NZ + way(n) * distance(n), NZ)

    def slot_of(n, hops):
        return (1 - way(n)) * REACH // 2 + hops - 1

    def to_relay(n):
        hops = distance(n) - REACH
        slot = slot_of(n, hops)
        return pltpu.make_async_remote_copy(
            src_ref=block.at[n],
            dst_ref=relay_in.at[slot],
            send_sem=block_send.at[n, 0],
            recv_sem=relay_recv.at[slot],
            device_id=at(lax.rem(z + NZ + way(n) * hops, NZ), x_lo),
            device_id_type=MESH,
        )

    def to_own(n, x):
        slot = slot_of(n, distance(n))
        return pltpu.make_async_remote_copy(
            src_ref=block.at[n, :, pl.ds(x * HALF, HALF)],
            dst_ref=z_in.at[slot, x_lo],
            send_sem=block_send.at[n, x],
            recv_sem=z_recv.at[slot, x_lo],
            device_id=at(tile_of(n), x),
            device_id_type=MESH,
        )

    my_half = pl.ds(pl.multiple_of(x_lo * HALF, HALF), HALF)
    to_x = pltpu.make_async_remote_copy(
        src_ref=block.at[NZ - 1, :, pl.ds(pl.multiple_of((1 - x_lo) * HALF, HALF), HALF)],
        dst_ref=x_in,
        send_sem=block_send.at[NZ - 1, 0],
        recv_sem=x_recv,
        device_id=at(z, 1 - x_lo),
        device_id_type=MESH,
    )

    def received(slot, x):
        pltpu.make_async_remote_copy(
            src_ref=block.at[0, :, pl.ds(0, HALF)],
            dst_ref=z_in.at[slot, x],
            send_sem=block_send.at[0, 0],
            recv_sem=z_recv.at[slot, x],
            device_id=at(z, 1 - x_lo),
            device_id_type=MESH,
        ).wait_recv()
        return z_in[slot, x].astype(F32)

    def interpolate(n, i):
        off = pl.multiple_of(tile_of(n) * TILE, TILE)
        for v in range(V):
            columns = jnp.dot(lhs[v], coarse[v, :, pl.ds(off, TILE)], preferred_element_type=F32)
            total = None
            for b in range(PARTS):
                weights = jnp.broadcast_to(fine[b, v : v + 1, pl.ds(off, TILE)], (2 * R, TILE))
                term = columns[b * 2 * R : (b + 1) * 2 * R] * weights
                total = term if total is None else total + term
            planes[i, v * 2 * R : (v + 1) * 2 * R, :] = total

    def picked(n, i):
        part[i] = jnp.dot(pick[tile_of(n)], planes[i].astype(BF16), preferred_element_type=F32)
        block[n] = part[i].astype(BF16)

    def step(m, carry):
        for i in range(2):
            interpolate(2 * m + i, i)
        for i in range(2):
            picked(2 * m + i, i)
        for i in range(2):
            n = 2 * m + i

            @pl.when(n < FAR)
            def _():
                to_relay(n).start()

            @pl.when(jnp.logical_and(n >= FAR, n < FAR + 2))
            def _():
                own[1 - i] = part[i]

            @pl.when(jnp.logical_and(n >= FAR + 2, n < NZ - 1))
            def _():
                for x in range(2):
                    to_own(n, x).start()

        return carry

    lax.fori_loop(0, NZ // 2, step, 0)
    to_x.start()

    for n, sources in ((FAR, (5, 3, 1)), (FAR + 1, (6, 4, 2, 0))):
        total = own[n - FAR]
        for source in sources:
            to_relay(source).wait_recv()
            total += relay_in[slot_of(source, distance(source) - REACH)].astype(F32)
        block[n] = total.astype(BF16)
        for x in range(2):
            to_own(n, x).start()

    def far_sent(n, carry):
        to_relay(n).wait_send()
        return carry

    def sent(n, carry):
        for x in range(2):
            to_own(n, x).wait_send()
        return carry

    lax.fori_loop(0, FAR, far_sent, 0)
    lax.fori_loop(FAR + 2, NZ - 1, sent, 0)

    to_x.wait_recv()
    total = part[1, :, my_half] + x_in[...].astype(F32)
    for n in (*range(FAR + 2, NZ - 1), FAR, FAR + 1):
        for x in range(2):
            total += received(slot_of(n, distance(n)), x)
    out_ref[...] = total * (1.0 / math.sqrt(V * lax.axis_size("view")))

    lax.fori_loop(FAR, FAR + 2, sent, 0)
    to_x.wait_send()
    pair.wait_send()

    @pl.when(slab > 0)
    def _():
        down.wait_send()

    @pl.when(slab < last)
    def _():
        up.wait_send()


def on_device(projections, conj_index, conj_weight, row_index, col_index, col_frac):
    pix = NZ * TILE
    anywhere = pl.BlockSpec(memory_space=pl.ANY)
    dma = pltpu.SemaphoreType.DMA
    return pl.pallas_call(
        kernel,
        out_shape=jax.ShapeDtypeStruct((NZ, HALF), F32),
        in_specs=[anywhere] * 6,
        out_specs=pl.BlockSpec(memory_space=pltpu.VMEM),
        scratch_shapes=[
            pltpu.SMEM((V,), jnp.int32),
            pltpu.VMEM((V, R, W), BF16),
            pltpu.VMEM((V, W), F32),
            pltpu.VMEM((V, NZ, NZ), jnp.int32),
            pltpu.VMEM((V, pix), jnp.int32),
            pltpu.VMEM((V, pix), jnp.int32),
            pltpu.VMEM((V * R, W), F32),
            pltpu.VMEM((V * R, W), BF16),
            pltpu.VMEM((V * R, W), BF16),
            pltpu.VMEM((V * R, W), F32),
            pltpu.VMEM((V, W), F32),
            pltpu.VMEM((W, PARTS * LANES), BF16),
            pltpu.VMEM((V * R, PARTS * LANES), BF16),
            pltpu.VMEM((V * R, PARTS * LANES), BF16),
            pltpu.VMEM((PARTS, 2 * R * V, LANES), F32),
            pltpu.VMEM((V, PARTS * 2 * R, LANES), BF16),
            pltpu.VMEM((V, LANES, pix), BF16),
            pltpu.VMEM((PARTS, V, pix), F32),
            pltpu.VMEM((NZ, NZ, 2 * R * V), BF16),
            pltpu.VMEM((2, 2 * R * V, TILE), F32),
            pltpu.VMEM((2, NZ, TILE), F32),
            pltpu.VMEM((2, NZ, TILE), F32),
            pltpu.VMEM((NZ, NZ, TILE), BF16),
            pltpu.VMEM((NZ, HALF), BF16),
            pltpu.VMEM((2 * REACH, NZ, TILE), BF16),
            pltpu.VMEM((2 * REACH, 2, NZ, HALF), BF16),
            dma((6,)),
            dma((2,)),
            dma((2,)),
            dma((2,)),
            dma((NZ, 2)),
            dma,
            dma((2 * REACH,)),
            dma((2 * REACH, 2)),
        ],
        compiler_params=pltpu.CompilerParams(
            collective_id=0, has_side_effects=True, vmem_limit_bytes=56 * 2**20
        ),
        name="backproject",
    )(conj_index, projections, conj_weight, row_index, col_index, col_frac)


def solution(mesh):
    return jax.shard_map(
        on_device,
        mesh=mesh,
        in_specs=(
            P("view", "slab", None),
            P("view"),
            P("view", None),
            P("view", None, "slab"),
            P("view", None),
            P("view", None),
        ),
        out_specs=P("slab", "view"),
        check_vma=False,
    )
```

```python
import math

import jax
import jax.numpy as jnp
from jax import lax
from jax.experimental import pallas as pl
from jax.experimental.pallas import tpu as pltpu
from jax.sharding import PartitionSpec as P

MESH = pl.DeviceIdType.MESH
BF16 = jnp.bfloat16
F32 = jnp.float32

V = 8
R = 4
W = 736
NZ = 16
TILE = 1024
HALF = TILE // 2
STEP = 6
PARTS = STEP + 1
LANES = 128
REACH = 4
FAR = NZ // 2 - 1


def iota(shape, dim):
    return lax.broadcasted_iota(jnp.int32, shape, dim)


def hat(distance):
    return jnp.maximum(1.0 - jnp.abs(distance), 0.0)


def kernel(
    conj_hbm,
    proj_hbm,
    weight_hbm,
    rows_hbm,
    col_hbm,
    frac_hbm,
    out_ref,
    conj_ref,
    proj,
    weight,
    rowidx,
    col,
    frac,
    stage,
    mine,
    theirs,
    kept,
    mirror_weight,
    ramp,
    edge,
    edge_in,
    band,
    lhs,
    coarse,
    fine,
    pick,
    planes,
    part,
    own,
    block,
    x_in,
    relay_in,
    z_in,
    load_sem,
    pair_sem,
    halo_send,
    halo_recv,
    block_send,
    x_recv,
    relay_recv,
    z_recv,
):
    view, slab = lax.axis_index("view"), lax.axis_index("slab")
    z, x_lo = view // 2, lax.rem(view, 2)
    last = lax.axis_size("slab") - 1

    def at(zz, xx):
        return (zz * 2 + xx, slab)

    def z_peer(distance):
        return lax.rem(z + distance, NZ)

    barrier = pltpu.get_barrier_semaphore()

    def greet(*device):
        pl.semaphore_signal(barrier, inc=1, device_id=device, device_id_type=MESH)

    def greet_z(d, carry):
        for x in range(2):
            greet(*at(z_peer(d), x))
            greet(*at(z_peer(NZ - d), x))
        return carry

    partner = at(z_peer(NZ // 2), x_lo)
    greet(*partner)
    lax.fori_loop(1, REACH + 1, greet_z, 0)
    greet(*at(z, 1 - x_lo))

    @pl.when(slab > 0)
    def _():
        greet(view, slab - 1)

    @pl.when(slab < last)
    def _():
        greet(view, slab + 1)

    loads = [
        pltpu.make_async_copy(src, dst, load_sem.at[i])
        for i, (src, dst) in enumerate(
            (
                (proj_hbm, proj),
                (weight_hbm, weight),
                (rows_hbm, rowidx),
                (col_hbm, col),
                (frac_hbm, frac),
                (conj_hbm, conj_ref),
            )
        )
    ]
    for load in loads:
        load.start()

    loads[0].wait()
    for v in range(V):
        rows = proj[v].astype(F32)
        for r in range(R):
            stage[r * V + v : r * V + v + 1, :] = rows[r : r + 1]
    mine[...] = stage[...].astype(BF16)

    loads[3].wait()
    loads[4].wait()

    def prepare(tile, carry):
        off = pl.multiple_of(tile * TILE, TILE)
        k = col[:, pl.ds(off, TILE)].astype(F32)
        a = jnp.floor((k + 0.5) * (1.0 / STEP))
        place = k - a * STEP + frac[:, pl.ds(off, TILE)].astype(F32) * (1.0 / 256.0)
        for b in range(PARTS):
            fine[b, :, pl.ds(off, TILE)] = hat(place - b)
        lanes = iota((LANES, TILE), 0).astype(F32).astype(BF16)
        for v in range(V):
            coarse[v, :, pl.ds(off, TILE)] = hat(lanes - a[v : v + 1, :].astype(BF16)).astype(BF16)
        return carry

    early = jnp.where(z < 8, 12, jnp.where(z < 12, 7, 10))
    lax.fori_loop(0, early, prepare, 0)

    below, above = (slab > 0).astype(jnp.int32), (slab < last).astype(jnp.int32)
    pl.semaphore_wait(barrier, 4 * REACH + 2 + below + above)
    pair = pltpu.make_async_remote_copy(
        src_ref=mine,
        dst_ref=theirs,
        send_sem=pair_sem.at[0],
        recv_sem=pair_sem.at[1],
        device_id=partner,
        device_id_type=MESH,
    )
    pair.start()
    lax.fori_loop(early, NZ, prepare, 0)

    for b in range(PARTS):
        column = STEP * iota((W, LANES), 1) + b
        offset = column + iota((W, LANES), 0) - (W - 1)
        square = (offset * offset).astype(F32)
        odd = -1.0 / (math.pi * math.pi * jnp.maximum(square, 1.0))
        value = jnp.where(offset == 0, 0.25, jnp.where((offset & 1) == 1, odd, 0.0))
        ramp[:, b * LANES : (b + 1) * LANES] = jnp.where(column < W, value, 0.0).astype(BF16)

    flip = jnp.where(iota((W, W), 0) + iota((W, W), 1) == W - 1, 1.0, 0.0).astype(BF16)
    loads[1].wait()
    whole = weight[...]
    high = whole.astype(BF16).astype(F32)
    middle = (whole - high).astype(BF16).astype(F32)
    low = (whole - high - middle).astype(BF16).astype(F32)
    split = jnp.concatenate([high, middle, low], axis=0).astype(BF16)
    flipped = jnp.dot(split, flip, preferred_element_type=F32)
    mirror_weight[...] = flipped[0:V] + flipped[V : 2 * V] + flipped[2 * V : 3 * V]
    share = jnp.concatenate([mirror_weight[...]] * R, axis=0)

    kept[...] = (1.0 - share) * jnp.dot(mine[...], flip, preferred_element_type=F32)

    loads[2].wait()
    for t in range(NZ):
        blocks = []
        for v in range(V):
            wanted = jnp.broadcast_to(rowidx[v, t : t + 1, :], (2 * R, NZ))
            blocks.append(jnp.where(wanted == iota((2 * R, NZ), 0), 1.0, 0.0))
        pick[t] = jnp.concatenate(blocks, axis=0).T.astype(BF16)

    row, other = iota((V * R, V * R), 0), iota((V * R, V * R), 1)
    conj = jnp.zeros((V * R, V * R), jnp.int32)
    loads[5].wait()
    for v in range(V):
        conj = jnp.where((row & (V - 1)) == v, conj_ref[v], conj)
    same_row = (row >> 3) == (other >> 3)
    select = jnp.where(jnp.logical_and(same_row, (other & (V - 1)) == conj), 1.0, 0.0).astype(BF16)
    pair.wait_recv()
    chosen = jnp.dot(select, theirs[...], preferred_element_type=F32)
    blended = (kept[...] + share * chosen).astype(BF16)
    edge[...] = jnp.dot(blended, ramp[...], preferred_element_type=F32).astype(BF16)

    half = R * V // 2
    first_rows, last_rows = pl.ds(0, half), pl.ds(half, half)

    def halo_copy(i, src, dst, to):
        return pltpu.make_async_remote_copy(
            src_ref=edge.at[src],
            dst_ref=edge_in.at[dst],
            send_sem=halo_send.at[i],
            recv_sem=halo_recv.at[i],
            device_id=(view, to),
            device_id_type=MESH,
        )

    down = halo_copy(0, first_rows, last_rows, jnp.maximum(slab - 1, 0))
    up = halo_copy(1, last_rows, first_rows, jnp.minimum(slab + 1, last))

    @pl.when(slab > 0)
    def _():
        down.start()

    @pl.when(slab < last)
    def _():
        up.start()

    @pl.when(slab == 0)
    def _():
        edge_in[first_rows, :] = jnp.zeros((half, PARTS * LANES), BF16)

    @pl.when(slab == last)
    def _():
        edge_in[last_rows, :] = jnp.zeros((half, PARTS * LANES), BF16)

    inner = edge[...].astype(F32)
    for b in range(PARTS):
        band[b, half : half + R * V, :] = inner[:, b * LANES : (b + 1) * LANES]

    @pl.when(slab < last)
    def _():
        down.wait_recv()

    @pl.when(slab > 0)
    def _():
        up.wait_recv()

    outer = edge_in[...].astype(F32)
    for b in range(PARTS):
        band[b, 0:half, :] = outer[0:half, b * LANES : (b + 1) * LANES]
        band[b, half + R * V :, :] = outer[half:, b * LANES : (b + 1) * LANES]

    for v in range(V):
        lhs[v] = jnp.concatenate(
            [band[b, pl.ds(v, 2 * R, stride=V), :] for b in range(PARTS)], axis=0
        ).astype(BF16)

    def way(n):
        return 1 - 2 * lax.rem(n, 2)

    def distance(n):
        return NZ // 2 - (n + 1) // 2

    def tile_of(n):
        return lax.rem(z + NZ + way(n) * distance(n), NZ)

    def slot_of(n, hops):
        return (1 - way(n)) * REACH // 2 + hops - 1

    def to_relay(n):
        hops = distance(n) - REACH
        slot = slot_of(n, hops)
        return pltpu.make_async_remote_copy(
            src_ref=block.at[n],
            dst_ref=relay_in.at[slot],
            send_sem=block_send.at[n, 0],
            recv_sem=relay_recv.at[slot],
            device_id=at(lax.rem(z + NZ + way(n) * hops, NZ), x_lo),
            device_id_type=MESH,
        )

    def to_own(n, x):
        slot = slot_of(n, distance(n))
        return pltpu.make_async_remote_copy(
            src_ref=block.at[n, :, pl.ds(x * HALF, HALF)],
            dst_ref=z_in.at[slot, x_lo],
            send_sem=block_send.at[n, x],
            recv_sem=z_recv.at[slot, x_lo],
            device_id=at(tile_of(n), x),
            device_id_type=MESH,
        )

    my_half = pl.ds(pl.multiple_of(x_lo * HALF, HALF), HALF)
    to_x = pltpu.make_async_remote_copy(
        src_ref=block.at[NZ - 1, :, pl.ds(pl.multiple_of((1 - x_lo) * HALF, HALF), HALF)],
        dst_ref=x_in,
        send_sem=block_send.at[NZ - 1, 0],
        recv_sem=x_recv,
        device_id=at(z, 1 - x_lo),
        device_id_type=MESH,
    )

    def received(slot, x):
        pltpu.make_async_remote_copy(
            src_ref=block.at[0, :, pl.ds(0, HALF)],
            dst_ref=z_in.at[slot, x],
            send_sem=block_send.at[0, 0],
            recv_sem=z_recv.at[slot, x],
            device_id=at(z, 1 - x_lo),
            device_id_type=MESH,
        ).wait_recv()
        return z_in[slot, x].astype(F32)

    def interpolate(n, i):
        off = pl.multiple_of(tile_of(n) * TILE, TILE)
        for v in range(V):
            columns = jnp.dot(lhs[v], coarse[v, :, pl.ds(off, TILE)], preferred_element_type=F32)
            total = None
            for b in range(PARTS):
                weights = jnp.broadcast_to(fine[b, v : v + 1, pl.ds(off, TILE)], (2 * R, TILE))
                term = columns[b * 2 * R : (b + 1) * 2 * R] * weights
                total = term if total is None else total + term
            planes[i, v * 2 * R : (v + 1) * 2 * R, :] = total

    def picked(n, i):
        part[i] = jnp.dot(pick[tile_of(n)], planes[i].astype(BF16), preferred_element_type=F32)
        block[n] = part[i].astype(BF16)

    def step(m, carry):
        for i in range(2):
            interpolate(2 * m + i, i)
        for i in range(2):
            picked(2 * m + i, i)
        for i in range(2):
            n = 2 * m + i

            @pl.when(n < FAR)
            def _():
                to_relay(n).start()

            @pl.when(jnp.logical_and(n >= FAR, n < FAR + 2))
            def _():
                own[1 - i] = part[i]

            @pl.when(jnp.logical_and(n >= FAR + 2, n < NZ - 1))
            def _():
                for x in range(2):
                    to_own(n, x).start()

        return carry

    lax.fori_loop(0, NZ // 2, step, 0)
    to_x.start()

    def relay(n):
        total = own[n - FAR]
        for source in range(n - 2, -1, -2):
            to_relay(source).wait_recv()
            total += relay_in[slot_of(source, distance(source) - REACH)].astype(F32)
        block[n] = total.astype(BF16)
        for x in range(2):
            to_own(n, x).start()

    upper = z >= NZ // 2

    @pl.when(upper)
    def _():
        relay(FAR + 1)
        relay(FAR)

    @pl.when(jnp.logical_not(upper))
    def _():
        relay(FAR)
        relay(FAR + 1)

    def far_sent(n, carry):
        to_relay(n).wait_send()
        return carry

    def sent(n, carry):
        for x in range(2):
            to_own(n, x).wait_send()
        return carry

    lax.fori_loop(0, FAR, far_sent, 0)
    lax.fori_loop(FAR + 2, NZ - 1, sent, 0)

    to_x.wait_recv()
    total = part[1, :, my_half] + x_in[...].astype(F32)
    for n in (*range(FAR + 2, NZ - 1), FAR, FAR + 1):
        for x in range(2):
            total += received(slot_of(n, distance(n)), x)
    out_ref[...] = total * (1.0 / math.sqrt(V * lax.axis_size("view")))

    lax.fori_loop(FAR, FAR + 2, sent, 0)
    to_x.wait_send()
    pair.wait_send()

    @pl.when(slab > 0)
    def _():
        down.wait_send()

    @pl.when(slab < last)
    def _():
        up.wait_send()


def on_device(projections, conj_index, conj_weight, row_index, col_index, col_frac):
    pix = NZ * TILE
    anywhere = pl.BlockSpec(memory_space=pl.ANY)
    dma = pltpu.SemaphoreType.DMA
    return pl.pallas_call(
        kernel,
        out_shape=jax.ShapeDtypeStruct((NZ, HALF), F32),
        in_specs=[anywhere] * 6,
        out_specs=pl.BlockSpec(memory_space=pltpu.VMEM),
        scratch_shapes=[
            pltpu.SMEM((V,), jnp.int32),
            pltpu.VMEM((V, R, W), BF16),
            pltpu.VMEM((V, W), F32),
            pltpu.VMEM((V, NZ, NZ), jnp.int32),
            pltpu.VMEM((V, pix), jnp.int32),
            pltpu.VMEM((V, pix), jnp.int32),
            pltpu.VMEM((V * R, W), F32),
            pltpu.VMEM((V * R, W), BF16),
            pltpu.VMEM((V * R, W), BF16),
            pltpu.VMEM((V * R, W), F32),
            pltpu.VMEM((V, W), F32),
            pltpu.VMEM((W, PARTS * LANES), BF16),
            pltpu.VMEM((V * R, PARTS * LANES), BF16),
            pltpu.VMEM((V * R, PARTS * LANES), BF16),
            pltpu.VMEM((PARTS, 2 * R * V, LANES), F32),
            pltpu.VMEM((V, PARTS * 2 * R, LANES), BF16),
            pltpu.VMEM((V, LANES, pix), BF16),
            pltpu.VMEM((PARTS, V, pix), F32),
            pltpu.VMEM((NZ, NZ, 2 * R * V), BF16),
            pltpu.VMEM((2, 2 * R * V, TILE), F32),
            pltpu.VMEM((2, NZ, TILE), F32),
            pltpu.VMEM((2, NZ, TILE), F32),
            pltpu.VMEM((NZ, NZ, TILE), BF16),
            pltpu.VMEM((NZ, HALF), BF16),
            pltpu.VMEM((2 * REACH, NZ, TILE), BF16),
            pltpu.VMEM((2 * REACH, 2, NZ, HALF), BF16),
            dma((6,)),
            dma((2,)),
            dma((2,)),
            dma((2,)),
            dma((NZ, 2)),
            dma,
            dma((2 * REACH,)),
            dma((2 * REACH, 2)),
        ],
        compiler_params=pltpu.CompilerParams(
            collective_id=0, has_side_effects=True, vmem_limit_bytes=56 * 2**20
        ),
        name="backproject",
    )(conj_index, projections, conj_weight, row_index, col_index, col_frac)


def solution(mesh):
    return jax.shard_map(
        on_device,
        mesh=mesh,
        in_specs=(
            P("view", "slab", None),
            P("view"),
            P("view", None),
            P("view", None, "slab"),
            P("view", None),
            P("view", None),
        ),
        out_specs=P("slab", "view"),
        check_vma=False,
    )
```
